32 devices in a mesh: groups: 2 (over x), srow: 8 (over z, y), scol: 2 (over core).
Axes of the slice: x: 2, y: 2, z: 4, core: 2. Of those that a mesh axis runs over, the one named last changes fastest.
Arguments:
- field_in: bfloat16 [256, 4096], P(('groups', 'srow'), 'scol'), parts along dimension 0, may hold values from -6 to 6
- cotangent: bfloat16 [256, 4096], P('groups', 'srow'), parts along dimension 0, may hold values from -6 to 6
- tile_vals: bfloat16 [16, 64, 128, 128], P(('groups', 'srow'), 'scol'), parts along dimension 0, may hold values from -0.1875 to 0.1875
- tile_rows: int32 [16, 64], P(('groups', 'srow'), 'scol'), parts along dimension 0, may hold values from 0 to 31, as said below
- tile_cols: int32 [16, 64], P('groups', 'scol'), parts along dimension 0, may hold values from 0 to 31, as said below
- lag_steps: int32 [4], P('groups'), parts along dimension 0, may hold values from 1 to 24, as said below
- ar_coef: float32 [6, 128], P('groups'), parts along dimension 0, may hold values from -1 to 1
Outputs:
- forward_out: float32 [256, 4096], P(('groups', 'scol'), 'srow'), parts along dimension 0
- adjoint_out: float32 [256, 4096], P(('groups', 'srow'), 'scol'), parts along dimension 0
The draws below stay inside these ranges and needn't reach their ends.
There are 2 independent parts, one for each index of `groups`. The reference program is written for one: setup_inputs(seed, part) draws one part's arguments, and reference() takes and returns one part's arrays. A program takes and returns all parts, laid end to end along the dimension named above; each array names one. Nothing has to cross between parts.
Inputs may be any that keep to these rules, and one draw needn't show every extreme that they name: `tile_rows`: the tiles of device (r, c), entries [r, c * 32] to [r, c * 32 + 31], lie in row blocks r * 4 to r * 4 + 3, each such row block holding exactly 8 of them. `tile_cols`: entries [., c * 32 + k] lie in column blocks c * 16 to c * 16 + 15; every column block has at least one tile. lag_steps[0] < lag_steps[1] = 24.
All inputs are finite; a program needn't handle non-finite values.
Results may differ from the reference program's by a relative error of at most 0.0029.
Values may be sent and summed in bfloat16 or wider, within the bound.
A program may use at most 128 MiB of HBM per device.

```python
import jax
import jax.numpy as jnp
from jax import lax

BS = 128
TPRB = 8
RBD = 4
TD = 16
MAXLAG = 24
NB = 32
NS = 4096
TPD = 32
NT = 128
N_SROW = 8
N_SCOL = 2


def draw_tile_rows(key, part):
    key = jax.random.fold_in(key, 11)
    subkeys = jax.random.split(key, N_SROW * N_SCOL)

    def shuffle(subkey):
        return jax.random.permutation(subkey, TPD)
    shuffles = jax.vmap(shuffle)(subkeys).reshape(N_SROW, N_SCOL * TPD)
    base_rows = jnp.arange(N_SROW, dtype=jnp.int32)[:, None] * RBD
    return (base_rows + shuffles % RBD).astype(jnp.int32)


def draw_tile_cols(key, part):
    key = jax.random.fold_in(key, 23)
    col_range = NB // N_SCOL
    subkeys = jax.random.split(key, N_SCOL)

    def shuffle(subkey):
        return jax.random.permutation(subkey, col_range)
    shuffles = jax.vmap(shuffle)(subkeys)
    position = (jnp.arange(N_SROW, dtype=jnp.int32)[:, None] * TPD + jnp.arange(TPD, dtype=jnp.int32)[None, :]) % col_range
    chosen = shuffles[:, position]
    offsets = jnp.arange(N_SCOL, dtype=jnp.int32)[:, None, None] * col_range
    chosen = jnp.transpose(chosen + offsets, (1, 0, 2))
    return chosen.reshape(N_SROW, N_SCOL * TPD).astype(jnp.int32)


def draw_lag_steps(key, part):
    key = jax.random.fold_in(key, 37)
    first_lag = jax.random.randint(key, (1,), 1, MAXLAG, dtype=jnp.int32)
    return jnp.concatenate([first_lag, jnp.full((1,), MAXLAG, jnp.int32)], 0)


def block_scale(own_key, dims, shards, smallest, high):
    def one(axis_at, blocks):
        heights = jax.random.uniform(jax.random.fold_in(jax.random.fold_in(own_key, 6), axis_at), (blocks,), jnp.float32, smallest / len(shards), high / len(shards))
        return jnp.repeat(jnp.exp(heights), dims[axis_at] // blocks).reshape((-1,) + (1,) * (len(dims) - axis_at - 1))

    factor_of = one(*shards[0])
    for cut in shards[1:]:
        factor_of = factor_of * one(*cut)
    return factor_of


def noise(key, extent, deviation, most, cuts=(), held_as=jnp.bfloat16):
    result = deviation * jax.random.normal(key, extent, jnp.float32)
    if cuts:
        result = result * block_scale(key, extent, cuts, -0.22, 0.18)
    return jnp.clip(result, -most, most).astype(held_as)


def setup_inputs(seed: int = 0, part: int = 0) -> dict:
    streams_of = jax.random.split(jax.random.key(seed), 8)
    own_keys = jax.random.split(jax.random.fold_in(streams_of[7], part), 8)
    field_in = noise(own_keys[0], (NT, NS), 1.0, 6.0, ((0, 8), (1, 2)))
    cotangent = noise(own_keys[1], (NT, NS), 1.0, 6.0, ((1, 8),))
    tile_vals = noise(own_keys[2], (N_SROW, N_SCOL * TPD, BS, BS), (BS * TPRB) ** -0.5, 0.1875, ((0, 8), (1, 2)))
    tile_rows = draw_tile_rows(jax.random.fold_in(jax.random.fold_in(streams_of[7], part), 71), part)
    tile_cols = draw_tile_cols(jax.random.fold_in(jax.random.fold_in(streams_of[7], part), 71), part)
    lag_steps = draw_lag_steps(jax.random.fold_in(jax.random.fold_in(streams_of[7], part), 71), part)
    ar_coef = jnp.clip(jax.random.uniform(own_keys[6], (3, NT), jnp.float32, -1.0, 1.0), -1.0, 1.0)
    return dict(field_in=field_in, cotangent=cotangent, tile_vals=tile_vals, tile_rows=tile_rows, tile_cols=tile_cols, lag_steps=lag_steps, ar_coef=ar_coef)


def space_forward(slab, tile_mats, row_ids, col_ids):
    hours = slab.shape[0]
    blocks = slab.reshape(hours, NB, BS).astype(jnp.float32)
    picked = jnp.take(blocks, col_ids, axis=1)
    products = jnp.einsum("tkd,ked->tke", picked, tile_mats, precision=lax.Precision.HIGHEST)
    summed = jax.ops.segment_sum(jnp.moveaxis(products, 1, 0), row_ids, num_segments=NB)
    return jnp.moveaxis(summed, 0, 1).reshape(hours, NS)


def space_adjoint(slab, tile_mats, row_ids, col_ids):
    hours = slab.shape[0]
    blocks = slab.reshape(hours, NB, BS).astype(jnp.float32)
    picked = jnp.take(blocks, row_ids, axis=1)
    products = jnp.einsum("tke,ked->tkd", picked, tile_mats, precision=lax.Precision.HIGHEST)
    summed = jax.ops.segment_sum(jnp.moveaxis(products, 1, 0), col_ids, num_segments=NB)
    return jnp.moveaxis(summed, 0, 1).reshape(hours, NS)


def delayed(values, lag):
    padded = jnp.concatenate([jnp.zeros((MAXLAG, values.shape[1]), values.dtype), values], 0)
    return lax.dynamic_slice_in_dim(padded, (MAXLAG - lag).astype(jnp.int32), NT, 0)


def advanced(values, lag):
    padded = jnp.concatenate([values, jnp.zeros((MAXLAG, values.shape[1]), values.dtype)], 0)
    return lax.dynamic_slice_in_dim(padded, lag.astype(jnp.int32), NT, 0)


def reference(field_in, cotangent, tile_vals, tile_rows, tile_cols, lag_steps, ar_coef):
    tile_mats = tile_vals.reshape(-1, BS, BS).astype(jnp.float32)
    row_ids = tile_rows.reshape(-1)
    col_ids = tile_cols.reshape(-1)

    def forward_slab(slab):
        return space_forward(slab, tile_mats, row_ids, col_ids)

    def adjoint_slab(slab):
        return space_adjoint(slab, tile_mats, row_ids, col_ids)

    space_image = lax.map(forward_slab, field_in.reshape(N_SROW, TD, NS)).reshape(NT, NS).astype(jnp.bfloat16)
    image_wide = space_image.astype(jnp.float32)
    forward_out = (ar_coef[0][:, None] * image_wide
                   + ar_coef[1][:, None] * delayed(image_wide, lag_steps[0])
                   + ar_coef[2][:, None] * delayed(image_wide, lag_steps[1]))
    cot_wide = cotangent.astype(jnp.float32)
    first_term = ar_coef[1][:, None] * cot_wide
    second_term = ar_coef[2][:, None] * cot_wide
    time_adjoint = (ar_coef[0][:, None] * cot_wide + advanced(first_term, lag_steps[0])
                    + advanced(second_term, lag_steps[1])).astype(jnp.bfloat16)
    adjoint_out = lax.map(adjoint_slab, time_adjoint.reshape(N_SROW, TD, NS)).reshape(NT, NS)
    return forward_out, adjoint_out
```

```python
import functools

import jax
import jax.numpy as jnp
from jax import lax
from jax.experimental import pallas as pl
from jax.experimental.pallas import tpu as pltpu
from jax.sharding import PartitionSpec as P

BS = 128
RBD = 4
TD = 16
MAXLAG = 24
F32 = jnp.float32
BF16 = jnp.bfloat16
MESH = pl.DeviceIdType.MESH


def shift_matrix(rows, cols, lag):
    at = lax.broadcasted_iota(jnp.int32, (rows, cols), 0) + lag
    return (lax.broadcasted_iota(jnp.int32, (rows, cols), 1) == at).astype(F32).astype(BF16)


def kernel(
    n,
    tiles,
    ncb,
    idx,
    coef,
    field,
    cot,
    mats,
    fwd_out,
    adj_out,
    field_all,
    field_v,
    field_send,
    cot_v,
    mats_v,
    adj_in,
    sums,
    adj_send,
    adj_recv,
    part,
    part_recv,
    local_sem,
    fs_sem,
    fr_sem,
    as_sem,
    ar_sem,
    ps_sem,
    pr_sem,
):
    hours = n * TD
    half = hours // 2
    ext = half + MAXLAG
    me = lax.axis_index("srow")
    mc = lax.axis_index("scol")
    o_row, o_col, o_prow, o_pcol = 0, tiles, 2 * tiles, 3 * tiles
    o_lrow = 4 * tiles
    o_lcol = o_lrow + RBD
    o_lag = o_lcol + ncb

    load_cot = pltpu.make_async_copy(cot, cot_v, local_sem.at[0])
    load_mats = pltpu.make_async_copy(mats, mats_v, local_sem.at[1])
    load_cot.start()
    load_mats.start()
    my_rows = pl.ds(pl.multiple_of(me * TD, TD), TD)
    load_own = pltpu.make_async_copy(field, field_v, local_sem.at[2])
    load_own.start()

    barrier = pltpu.get_barrier_semaphore()
    for i in range(1, n):
        pl.semaphore_signal(
            barrier, inc=1, device_id={"srow": lax.rem(me + i, n)}, device_id_type=MESH
        )
    pl.semaphore_signal(barrier, inc=1, device_id={"scol": 1 - mc}, device_id_type=MESH)
    load_own.wait()
    for b in range(ncb):
        block = field_v[:, b * BS : (b + 1) * BS]
        field_send[b] = block
        field_all[b, my_rows, :] = block
    pl.semaphore_wait(barrier, n)

    def rows_of(r):
        return pl.ds(pl.multiple_of(r * TD, TD), TD)

    def field_copy(dst, src):
        return pltpu.make_async_remote_copy(
            src_ref=field_send,
            dst_ref=field_all.at[:, rows_of(src), :],
            send_sem=fs_sem.at[dst],
            recv_sem=fr_sem.at[src],
            device_id={"srow": dst},
            device_id_type=MESH,
        )

    def adj_copy(dst, src):
        return pltpu.make_async_remote_copy(
            src_ref=adj_send.at[rows_of(dst), :],
            dst_ref=adj_recv.at[rows_of(src), :],
            send_sem=as_sem.at[dst],
            recv_sem=ar_sem.at[src],
            device_id={"srow": dst},
            device_id_type=MESH,
        )

    for i in range(1, n):
        field_copy(lax.rem(me + i, n), me).start()

    load_cot.wait()
    spread = coef[...]
    lag1 = idx[o_lag]
    early = cot_v[...]
    wide = early.astype(F32)
    later = jnp.dot(shift_matrix(hours, hours, lag1), early, preferred_element_type=F32)
    far = jnp.concatenate([wide[MAXLAG:], jnp.zeros((MAXLAG, RBD * BS), F32)], 0)
    adjoint = (
        spread[:, 0:1] * wide + spread[:, 3:4] * later + spread[:, 4:5] * far
    ).astype(BF16)
    for r in range(RBD):
        adj_in[r] = adjoint[:, r * BS : (r + 1) * BS]

    load_mats.wait()
    sums[0] = jnp.zeros((hours, BS), F32)

    def adj_step(k, carry):
        product = jnp.dot(adj_in[idx[o_row + k]], mats_v[k], preferred_element_type=F32)
        sums[k + 1] = sums[idx[o_pcol + k]] + product
        return carry

    lax.fori_loop(0, tiles, adj_step, 0, unroll=4)
    for b in range(ncb):
        adj_send[:, b * BS : (b + 1) * BS] = sums[idx[o_lcol + b]].astype(BF16)
    for i in range(1, n):
        adj_copy(lax.rem(me + i, n), me).start()

    for i in range(1, n):
        field_copy(me, lax.rem(me + n - i, n)).wait_recv()

    def fwd_step(k, carry):
        product = lax.dot_general(
            field_all[idx[o_col + k]], mats_v[k], (((1,), (1,)), ((), ())), preferred_element_type=F32
        )
        sums[k + 1] = sums[idx[o_prow + k]] + product
        return carry

    lax.fori_loop(0, tiles, fwd_step, 0, unroll=4)
    part[pl.ds(0, MAXLAG), :] = jnp.zeros((MAXLAG, RBD * BS), F32)
    for r in range(RBD):
        part[pl.ds(MAXLAG, hours), r * BS : (r + 1) * BS] = sums[idx[o_lrow + r]]
    exchange = pltpu.make_async_remote_copy(
        src_ref=part.at[pl.ds(pl.multiple_of((1 - mc) * half, 8), ext), :],
        dst_ref=part_recv,
        send_sem=ps_sem,
        recv_sem=pr_sem,
        device_id={"scol": 1 - mc},
        device_id_type=MESH,
    )
    exchange.start()
    exchange.wait_recv()
    own = part[pl.ds(pl.multiple_of(mc * half, 8), ext), :]
    value = (own + part_recv[...]).astype(BF16)
    spread = coef[pl.ds(pl.multiple_of(mc * half, 8), half), :]
    delayed = jnp.dot(
        shift_matrix(half, ext, MAXLAG - lag1), value, preferred_element_type=F32
    )
    value = value.astype(F32)
    fwd_out[...] = (
        spread[:, 0:1] * value[MAXLAG:] + spread[:, 1:2] * delayed + spread[:, 2:3] * value[:half]
    )

    adj_out[...] = adj_send[my_rows, :].astype(F32)
    for i in range(1, n):
        src = lax.rem(me + n - i, n)
        adj_copy(me, src).wait_recv()
        adj_out[...] += adj_recv[rows_of(src), :].astype(F32)

    exchange.wait_send()
    for i in range(1, n):
        dst = lax.rem(me + i, n)
        field_copy(dst, me).wait_send()
        adj_copy(dst, me).wait_send()


def body(field_in, cotangent, tile_vals, tile_rows, tile_cols, lag_steps, ar_coef):
    n = lax.axis_size("srow")
    row_index = lax.axis_index("srow")
    col_index = lax.axis_index("scol")
    tiles = tile_vals.shape[1]
    cols = field_in.shape[1]
    ncb = cols // BS
    hours = n * TD
    rows = tile_rows[0] - row_index * RBD
    own_cols = lax.dynamic_slice_in_dim(tile_cols, row_index, 1, 0)[0] - col_index * ncb
    place = jnp.arange(tiles, dtype=jnp.int32)
    earlier = place[None, :] < place[:, None]

    def chain(ids, blocks):
        same = (ids[:, None] == ids[None, :]) & earlier
        prev = jnp.max(jnp.where(same, place[None, :] + 1, 0), axis=1)
        which = jnp.arange(blocks, dtype=jnp.int32)[:, None] == ids[None, :]
        last = jnp.max(jnp.where(which, place[None, :] + 1, 0), axis=1)
        return prev, last

    prow, lrow = chain(rows, RBD)
    pcol, lcol = chain(own_cols, ncb)
    idx = jnp.concatenate([rows, own_cols, prow, pcol, lrow, lcol, lag_steps])
    padded = jnp.pad(ar_coef, ((0, 0), (0, MAXLAG)))
    ahead = lax.dynamic_slice_in_dim(padded[1], lag_steps[0], hours)
    spare = jnp.zeros((3, hours), F32)
    coef = jnp.concatenate([ar_coef, ahead[None], padded[2:3, MAXLAG:], spare]).T

    anyspace = pl.BlockSpec(memory_space=pl.ANY)
    vmem = pl.BlockSpec(memory_space=pltpu.VMEM)
    half = hours // 2
    wide = RBD * BS
    return pl.pallas_call(
        functools.partial(kernel, n, tiles, ncb),
        out_shape=(
            jax.ShapeDtypeStruct((half, wide), F32),
            jax.ShapeDtypeStruct((TD, cols), F32),
        ),
        in_specs=[pl.BlockSpec(memory_space=pltpu.SMEM), vmem, anyspace, anyspace, anyspace],
        out_specs=(vmem, vmem),
        scratch_shapes=[
            pltpu.VMEM((ncb, hours, BS), BF16),
            pltpu.VMEM((TD, cols), BF16),
            pltpu.VMEM((ncb, TD, BS), BF16),
            pltpu.VMEM((hours, wide), BF16),
            pltpu.VMEM((tiles, BS, BS), BF16),
            pltpu.VMEM((RBD, hours, BS), BF16),
            pltpu.VMEM((tiles + 1, hours, BS), F32),
            pltpu.VMEM((hours, cols), BF16),
            pltpu.VMEM((hours, cols), BF16),
            pltpu.VMEM((hours + MAXLAG, wide), F32),
            pltpu.VMEM((half + MAXLAG, wide), F32),
            pltpu.SemaphoreType.DMA((3,)),
            pltpu.SemaphoreType.DMA((n,)),
            pltpu.SemaphoreType.DMA((n,)),
            pltpu.SemaphoreType.DMA((n,)),
            pltpu.SemaphoreType.DMA((n,)),
            pltpu.SemaphoreType.DMA,
            pltpu.SemaphoreType.DMA,
        ],
        compiler_params=pltpu.CompilerParams(
            collective_id=0, has_side_effects=True, vmem_limit_bytes=58 * 1024 * 1024
        ),
        cost_estimate=pl.CostEstimate(
            flops=4 * tiles * hours * BS * BS, bytes_accessed=2 << 20, transcendentals=0
        ),
    )(idx, coef, field_in, cotangent, tile_vals[0])


def solution(mesh):
    in_specs = (
        P(("groups", "srow"), "scol"),
        P("groups", "srow"),
        P(("groups", "srow"), "scol", None, None),
        P(("groups", "srow"), "scol"),
        P("groups", "scol"),
        P("groups"),
        P("groups", None),
    )
    out_specs = (P(("groups", "scol"), "srow"), P(("groups", "srow"), "scol"))
    return jax.shard_map(body, mesh=mesh, in_specs=in_specs, out_specs=out_specs, check_vma=False)
```

```python
import functools

import jax
import jax.numpy as jnp
from jax import lax
from jax.experimental import pallas as pl
from jax.experimental.pallas import tpu as pltpu
from jax.sharding import PartitionSpec as P

BS = 128
RBD = 4
TD = 16
MAXLAG = 24
PAIR = 2
F32 = jnp.float32
BF16 = jnp.bfloat16
MESH = pl.DeviceIdType.MESH


def shift_matrix(rows, cols, lag):
    at = lax.broadcasted_iota(jnp.int32, (rows, cols), 0) + lag
    return (lax.broadcasted_iota(jnp.int32, (rows, cols), 1) == at).astype(F32).astype(BF16)


def kernel(
    n,
    tiles,
    ncb,
    idx,
    coef,
    field,
    cot,
    mats,
    fwd_out,
    adj_out,
    field_all,
    field_v,
    field_send,
    cot_v,
    mats_v,
    adj_in,
    sums,
    adj_part,
    adj_send,
    adj_recv,
    line_send,
    line_recv,
    part,
    part_recv,
    local_sem,
    fs_sem,
    fr_sem,
    fp_sem,
    as_sem,
    ar_sem,
    ls_sem,
    lr_sem,
    ps_sem,
    pr_sem,
):
    hours = n * TD
    half = hours // 2
    ext = half + MAXLAG
    me = lax.axis_index("srow")
    mc = lax.axis_index("scol")
    o_row, o_col, o_prow, o_pcol = 0, tiles, 2 * tiles, 3 * tiles
    o_lrow = 4 * tiles
    o_lcol = o_lrow + RBD
    o_lag = o_lcol + ncb

    load_cot = pltpu.make_async_copy(cot, cot_v, local_sem.at[0])
    load_mats = pltpu.make_async_copy(mats, mats_v, local_sem.at[1])
    load_cot.start()
    load_mats.start()
    my_rows = pl.ds(pl.multiple_of(me * TD, TD), TD)
    load_own = pltpu.make_async_copy(field, field_v, local_sem.at[2])
    load_own.start()

    nz = n // PAIR
    mz, my = me // PAIR, lax.rem(me, PAIR)
    peer = mz * PAIR + 1 - my

    def on_line(z):
        return lax.rem(mz + z + nz, nz) * PAIR + my

    barrier = pltpu.get_barrier_semaphore()
    for i in range(1, nz):
        pl.semaphore_signal(barrier, inc=1, device_id={"srow": on_line(i)}, device_id_type=MESH)
    pl.semaphore_signal(barrier, inc=1, device_id={"srow": peer}, device_id_type=MESH)
    pl.semaphore_signal(barrier, inc=1, device_id={"scol": 1 - mc}, device_id_type=MESH)
    load_own.wait()
    for b in range(ncb):
        block = field_v[:, b * BS : (b + 1) * BS]
        field_send[b] = block
        field_all[b, my_rows, :] = block
    pl.semaphore_wait(barrier, nz + 1)

    def rows_of(r):
        return pl.ds(pl.multiple_of(r * TD, TD), TD)

    def line_copy(dst, src):
        return pltpu.make_async_remote_copy(
            src_ref=field_send,
            dst_ref=field_all.at[:, rows_of(src), :],
            send_sem=fs_sem.at[dst],
            recv_sem=fr_sem.at[src],
            device_id={"srow": dst},
            device_id_type=MESH,
        )

    def peer_copy(src):
        return pltpu.make_async_remote_copy(
            src_ref=field_all.at[:, rows_of(src), :],
            dst_ref=field_all.at[:, rows_of(src), :],
            send_sem=fp_sem.at[src // PAIR],
            recv_sem=fr_sem.at[src],
            device_id={"srow": peer},
            device_id_type=MESH,
        )

    def adj_peer_copy(z):
        return pltpu.make_async_remote_copy(
            src_ref=adj_send.at[rows_of(z), :],
            dst_ref=adj_recv.at[rows_of(z), :],
            send_sem=as_sem.at[z],
            recv_sem=ar_sem.at[z],
            device_id={"srow": peer},
            device_id_type=MESH,
        )

    def adj_line_copy(dst, src):
        return pltpu.make_async_remote_copy(
            src_ref=line_send.at[rows_of(dst // PAIR), :],
            dst_ref=line_recv.at[rows_of(src // PAIR), :],
            send_sem=ls_sem.at[dst // PAIR],
            recv_sem=lr_sem.at[src // PAIR],
            device_id={"srow": dst},
            device_id_type=MESH,
        )

    for i in range(1, nz):
        line_copy(on_line(i), me).start()
    peer_copy(me).start()

    load_cot.wait()
    spread = coef[...]
    lag1 = idx[o_lag]
    early = cot_v[...]
    wide = early.astype(F32)
    later = jnp.dot(shift_matrix(hours, hours, lag1), early, preferred_element_type=F32)
    far = jnp.concatenate([wide[MAXLAG:], jnp.zeros((MAXLAG, RBD * BS), F32)], 0)
    adjoint = (
        spread[:, 0:1] * wide + spread[:, 3:4] * later + spread[:, 4:5] * far
    ).astype(BF16)
    for r in range(RBD):
        adj_in[r] = adjoint[:, r * BS : (r + 1) * BS]

    load_mats.wait()
    sums[0] = jnp.zeros((hours, BS), F32)

    def adj_step(k, carry):
        product = jnp.dot(adj_in[idx[o_row + k]], mats_v[k], preferred_element_type=F32)
        sums[k + 1] = sums[idx[o_pcol + k]] + product
        return carry

    lax.fori_loop(0, tiles // 2, adj_step, 0, unroll=4)
    line_copy(me, on_line(-1)).wait_recv()
    peer_copy(on_line(-1)).start()
    lax.fori_loop(tiles // 2, tiles, adj_step, 0, unroll=4)
    for b in range(ncb):
        block = sums[idx[o_lcol + b]].reshape(nz, PAIR, TD, BS)
        at = slice(b * BS, (b + 1) * BS)
        mine = jnp.where(my == 0, block[:, 0], block[:, 1])
        other = jnp.where(my == 0, block[:, 1], block[:, 0])
        adj_part[:, at] = mine.reshape(half, BS)
        adj_send[:, at] = other.reshape(half, BS).astype(BF16)
    for i in range(2, nz):
        line_copy(me, on_line(-i)).wait_recv()
        peer_copy(on_line(-i)).start()
    for i in range(1, nz + 1):
        adj_peer_copy(lax.rem(mz + i, nz)).start()

    for i in range(nz):
        peer_copy(lax.rem(mz + nz - i, nz) * PAIR + 1 - my).wait_recv()

    def fwd_step(k, carry):
        product = lax.dot_general(
            field_all[idx[o_col + k]], mats_v[k], (((1,), (1,)), ((), ())), preferred_element_type=F32
        )
        sums[k + 1] = sums[idx[o_prow + k]] + product
        return carry

    lax.fori_loop(0, tiles, fwd_step, 0, unroll=4)
    part[pl.ds(0, MAXLAG), :] = jnp.zeros((MAXLAG, RBD * BS), F32)
    for r in range(RBD):
        part[pl.ds(MAXLAG, hours), r * BS : (r + 1) * BS] = sums[idx[o_lrow + r]]
    exchange = pltpu.make_async_remote_copy(
        src_ref=part.at[pl.ds(pl.multiple_of((1 - mc) * half, 8), ext), :],
        dst_ref=part_recv,
        send_sem=ps_sem,
        recv_sem=pr_sem,
        device_id={"scol": 1 - mc},
        device_id_type=MESH,
    )
    exchange.start()

    for i in range(1, nz):
        z = lax.rem(mz + i, nz)
        adj_peer_copy(z).wait_recv()
        total = adj_part[rows_of(z), :] + adj_recv[rows_of(z), :].astype(F32)
        line_send[rows_of(z), :] = total.astype(BF16)
        adj_line_copy(on_line(i), me).start()

    exchange.wait_recv()
    own = part[pl.ds(pl.multiple_of(mc * half, 8), ext), :]
    value = (own + part_recv[...]).astype(BF16)
    spread = coef[pl.ds(pl.multiple_of(mc * half, 8), half), :]
    delayed = jnp.dot(
        shift_matrix(half, ext, MAXLAG - lag1), value, preferred_element_type=F32
    )
    value = value.astype(F32)
    fwd_out[...] = (
        spread[:, 0:1] * value[MAXLAG:] + spread[:, 1:2] * delayed + spread[:, 2:3] * value[:half]
    )

    adj_peer_copy(mz).wait_recv()
    total = adj_part[rows_of(mz), :] + adj_recv[rows_of(mz), :].astype(F32)
    for i in range(1, nz):
        src = on_line(-i)
        adj_line_copy(me, src).wait_recv()
        total += line_recv[rows_of(src // PAIR), :].astype(F32)
    adj_out[...] = total

    exchange.wait_send()
    for i in range(1, nz):
        line_copy(on_line(i), me).wait_send()
        adj_line_copy(on_line(i), me).wait_send()
    for i in range(nz):
        peer_copy(on_line(-i)).wait_send()
        adj_peer_copy(lax.rem(mz + i, nz)).wait_send()


def body(field_in, cotangent, tile_vals, tile_rows, tile_cols, lag_steps, ar_coef):
    n = lax.axis_size("srow")
    row_index = lax.axis_index("srow")
    col_index = lax.axis_index("scol")
    tiles = tile_vals.shape[1]
    cols = field_in.shape[1]
    ncb = cols // BS
    hours = n * TD
    rows = tile_rows[0] - row_index * RBD
    own_cols = lax.dynamic_slice_in_dim(tile_cols, row_index, 1, 0)[0] - col_index * ncb
    place = jnp.arange(tiles, dtype=jnp.int32)
    earlier = place[None, :] < place[:, None]

    def chain(ids, blocks):
        same = (ids[:, None] == ids[None, :]) & earlier
        prev = jnp.max(jnp.where(same, place[None, :] + 1, 0), axis=1)
        which = jnp.arange(blocks, dtype=jnp.int32)[:, None] == ids[None, :]
        last = jnp.max(jnp.where(which, place[None, :] + 1, 0), axis=1)
        return prev, last

    prow, lrow = chain(rows, RBD)
    pcol, lcol = chain(own_cols, ncb)
    idx = jnp.concatenate([rows, own_cols, prow, pcol, lrow, lcol, lag_steps])
    padded = jnp.pad(ar_coef, ((0, 0), (0, MAXLAG)))
    ahead = lax.dynamic_slice_in_dim(padded[1], lag_steps[0], hours)
    spare = jnp.zeros((3, hours), F32)
    coef = jnp.concatenate([ar_coef, ahead[None], padded[2:3, MAXLAG:], spare]).T

    anyspace = pl.BlockSpec(memory_space=pl.ANY)
    vmem = pl.BlockSpec(memory_space=pltpu.VMEM)
    half = hours // 2
    nz = n // PAIR
    wide = RBD * BS
    return pl.pallas_call(
        functools.partial(kernel, n, tiles, ncb),
        out_shape=(
            jax.ShapeDtypeStruct((half, wide), F32),
            jax.ShapeDtypeStruct((TD, cols), F32),
        ),
        in_specs=[pl.BlockSpec(memory_space=pltpu.SMEM), vmem, anyspace, anyspace, anyspace],
        out_specs=(vmem, vmem),
        scratch_shapes=[
            pltpu.VMEM((ncb, hours, BS), BF16),
            pltpu.VMEM((TD, cols), BF16),
            pltpu.VMEM((ncb, TD, BS), BF16),
            pltpu.VMEM((hours, wide), BF16),
            pltpu.VMEM((tiles, BS, BS), BF16),
            pltpu.VMEM((RBD, hours, BS), BF16),
            pltpu.VMEM((tiles + 1, hours, BS), F32),
            pltpu.VMEM((half, cols), F32),
            pltpu.VMEM((half, cols), BF16),
            pltpu.VMEM((half, cols), BF16),
            pltpu.VMEM((half, cols), BF16),
            pltpu.VMEM((half, cols), BF16),
            pltpu.VMEM((hours + MAXLAG, wide), F32),
            pltpu.VMEM((half + MAXLAG, wide), F32),
            pltpu.SemaphoreType.DMA((3,)),
            pltpu.SemaphoreType.DMA((n,)),
            pltpu.SemaphoreType.DMA((n,)),
            pltpu.SemaphoreType.DMA((nz,)),
            pltpu.SemaphoreType.DMA((nz,)),
            pltpu.SemaphoreType.DMA((nz,)),
            pltpu.SemaphoreType.DMA((nz,)),
            pltpu.SemaphoreType.DMA((nz,)),
            pltpu.SemaphoreType.DMA,
            pltpu.SemaphoreType.DMA,
        ],
        compiler_params=pltpu.CompilerParams(
            collective_id=0, has_side_effects=True, vmem_limit_bytes=58 * 1024 * 1024
        ),
        cost_estimate=pl.CostEstimate(
            flops=4 * tiles * hours * BS * BS, bytes_accessed=2 << 20, transcendentals=0
        ),
    )(idx, coef, field_in, cotangent, tile_vals[0])


def solution(mesh):
    in_specs = (
        P(("groups", "srow"), "scol"),
        P("groups", "srow"),
        P(("groups", "srow"), "scol", None, None),
        P(("groups", "srow"), "scol"),
        P("groups", "scol"),
        P("groups"),
        P("groups", None),
    )
    out_specs = (P(("groups", "scol"), "srow"), P(("groups", "srow"), "scol"))
    return jax.shard_map(body, mesh=mesh, in_specs=in_specs, out_specs=out_specs, check_vma=False)
```

```python
import functools

import jax
import jax.numpy as jnp
from jax import lax
from jax.experimental import pallas as pl
from jax.experimental.pallas import tpu as pltpu
from jax.sharding import PartitionSpec as P

BS = 128
RBD = 4
TD = 16
MAXLAG = 24
PAIR = 2
F32 = jnp.float32
BF16 = jnp.bfloat16
MESH = pl.DeviceIdType.MESH


def shift_matrix(rows, cols, lag):
    at = lax.broadcasted_iota(jnp.int32, (rows, cols), 0) + lag
    return (lax.broadcasted_iota(jnp.int32, (rows, cols), 1) == at).astype(F32).astype(BF16)


def kernel(
    n,
    tiles,
    ncb,
    idx,
    coef,
    field,
    cot,
    mats,
    fwd_out,
    adj_out,
    field_all,
    field_v,
    field_send,
    cot_v,
    mats_v,
    adj_in,
    sums,
    adj_part,
    adj_send,
    adj_recv,
    line_send,
    line_recv,
    part,
    part_recv,
    local_sem,
    fs_sem,
    fr_sem,
    fp_sem,
    as_sem,
    ar_sem,
    ls_sem,
    lr_sem,
    ps_sem,
    pr_sem,
):
    hours = n * TD
    half = hours // 2
    ext = half + MAXLAG
    me = lax.axis_index("srow")
    mc = lax.axis_index("scol")
    o_row, o_col, o_prow, o_pcol = 0, tiles, 2 * tiles, 3 * tiles
    o_lrow = 4 * tiles
    o_lcol = o_lrow + RBD
    o_lag = o_lcol + ncb

    load_cot = pltpu.make_async_copy(cot, cot_v, local_sem.at[0])
    load_mats = pltpu.make_async_copy(mats, mats_v, local_sem.at[1])
    load_cot.start()
    load_mats.start()
    my_rows = pl.ds(pl.multiple_of(me * TD, TD), TD)
    load_own = pltpu.make_async_copy(field, field_v, local_sem.at[2])
    load_own.start()

    nz = n // PAIR
    mz, my = me // PAIR, lax.rem(me, PAIR)
    peer = mz * PAIR + 1 - my

    def on_line(z):
        return lax.rem(mz + z + nz, nz) * PAIR + my

    barrier = pltpu.get_barrier_semaphore()
    for i in range(1, nz):
        pl.semaphore_signal(barrier, inc=1, device_id={"srow": on_line(i)}, device_id_type=MESH)
    pl.semaphore_signal(barrier, inc=1, device_id={"srow": peer}, device_id_type=MESH)
    pl.semaphore_signal(barrier, inc=1, device_id={"scol": 1 - mc}, device_id_type=MESH)
    load_own.wait()
    for b in range(ncb):
        block = field_v[:, b * BS : (b + 1) * BS]
        field_send[b] = block
        field_all[b, my_rows, :] = block
    pl.semaphore_wait(barrier, nz + 1)

    def rows_of(r):
        return pl.ds(pl.multiple_of(r * TD, TD), TD)

    def line_copy(dst, src):
        return pltpu.make_async_remote_copy(
            src_ref=field_send,
            dst_ref=field_all.at[:, rows_of(src), :],
            send_sem=fs_sem.at[dst],
            recv_sem=fr_sem.at[src],
            device_id={"srow": dst},
            device_id_type=MESH,
        )

    def peer_copy(src):
        return pltpu.make_async_remote_copy(
            src_ref=field_all.at[:, rows_of(src), :],
            dst_ref=field_all.at[:, rows_of(src), :],
            send_sem=fp_sem.at[src // PAIR],
            recv_sem=fr_sem.at[src],
            device_id={"srow": peer},
            device_id_type=MESH,
        )

    def adj_peer_copy(z):
        return pltpu.make_async_remote_copy(
            src_ref=adj_send.at[rows_of(z), :],
            dst_ref=adj_recv.at[rows_of(z), :],
            send_sem=as_sem.at[z],
            recv_sem=ar_sem.at[z],
            device_id={"srow": peer},
            device_id_type=MESH,
        )

    def adj_line_copy(dst, src):
        return pltpu.make_async_remote_copy(
            src_ref=line_send.at[rows_of(dst // PAIR), :],
            dst_ref=line_recv.at[rows_of(src // PAIR), :],
            send_sem=ls_sem.at[dst // PAIR],
            recv_sem=lr_sem.at[src // PAIR],
            device_id={"srow": dst},
            device_id_type=MESH,
        )

    for i in range(1, nz):
        line_copy(on_line(i), me).start()
    peer_copy(me).start()

    load_cot.wait()
    spread = coef[...]
    lag1 = idx[o_lag]
    early = cot_v[...]
    wide = early.astype(F32)
    later = jnp.dot(shift_matrix(hours, hours, lag1), early, preferred_element_type=F32)
    far = jnp.concatenate([wide[MAXLAG:], jnp.zeros((MAXLAG, RBD * BS), F32)], 0)
    adjoint = (
        spread[:, 0:1] * wide + spread[:, 3:4] * later + spread[:, 4:5] * far
    ).astype(BF16)
    for r in range(RBD):
        adj_in[r] = adjoint[:, r * BS : (r + 1) * BS]

    load_mats.wait()
    sums[0] = jnp.zeros((hours, BS), F32)

    def adj_step(k, carry):
        product = jnp.dot(adj_in[idx[o_row + k]], mats_v[k], preferred_element_type=F32)
        sums[k + 1] = sums[idx[o_pcol + k]] + product
        return carry

    lax.fori_loop(0, tiles, adj_step, 0, unroll=4)
    for b in range(ncb):
        block = sums[idx[o_lcol + b]].reshape(nz, PAIR, TD, BS)
        at = slice(b * BS, (b + 1) * BS)
        mine = jnp.where(my == 0, block[:, 0], block[:, 1])
        other = jnp.where(my == 0, block[:, 1], block[:, 0])
        adj_part[:, at] = mine.reshape(half, BS)
        adj_send[:, at] = other.reshape(half, BS).astype(BF16)
    for i in range(1, nz + 1):
        adj_peer_copy(lax.rem(mz + i, nz)).start()
    for i in range(1, nz):
        line_copy(me, on_line(-i)).wait_recv()
        peer_copy(on_line(-i)).start()

    for i in range(1, nz):
        z = lax.rem(mz + i, nz)
        adj_peer_copy(z).wait_recv()
        total = adj_part[rows_of(z), :] + adj_recv[rows_of(z), :].astype(F32)
        line_send[rows_of(z), :] = total.astype(BF16)
        adj_line_copy(on_line(i), me).start()

    for i in range(nz):
        peer_copy(lax.rem(mz + nz - i, nz) * PAIR + 1 - my).wait_recv()

    def fwd_step(k, carry):
        product = lax.dot_general(
            field_all[idx[o_col + k]], mats_v[k], (((1,), (1,)), ((), ())), preferred_element_type=F32
        )
        sums[k + 1] = sums[idx[o_prow + k]] + product
        return carry

    lax.fori_loop(0, tiles, fwd_step, 0, unroll=4)
    part[pl.ds(0, MAXLAG), :] = jnp.zeros((MAXLAG, RBD * BS), F32)
    for r in range(RBD):
        part[pl.ds(MAXLAG, hours), r * BS : (r + 1) * BS] = sums[idx[o_lrow + r]]
    exchange = pltpu.make_async_remote_copy(
        src_ref=part.at[pl.ds(pl.multiple_of((1 - mc) * half, 8), ext), :],
        dst_ref=part_recv,
        send_sem=ps_sem,
        recv_sem=pr_sem,
        device_id={"scol": 1 - mc},
        device_id_type=MESH,
    )
    exchange.start()
    exchange.wait_recv()
    own = part[pl.ds(pl.multiple_of(mc * half, 8), ext), :]
    value = (own + part_recv[...]).astype(BF16)
    spread = coef[pl.ds(pl.multiple_of(mc * half, 8), half), :]
    delayed = jnp.dot(
        shift_matrix(half, ext, MAXLAG - lag1), value, preferred_element_type=F32
    )
    value = value.astype(F32)
    fwd_out[...] = (
        spread[:, 0:1] * value[MAXLAG:] + spread[:, 1:2] * delayed + spread[:, 2:3] * value[:half]
    )

    adj_peer_copy(mz).wait_recv()
    total = adj_part[rows_of(mz), :] + adj_recv[rows_of(mz), :].astype(F32)
    for i in range(1, nz):
        src = on_line(-i)
        adj_line_copy(me, src).wait_recv()
        total += line_recv[rows_of(src // PAIR), :].astype(F32)
    adj_out[...] = total

    exchange.wait_send()
    for i in range(1, nz):
        line_copy(on_line(i), me).wait_send()
        adj_line_copy(on_line(i), me).wait_send()
    for i in range(nz):
        peer_copy(on_line(-i)).wait_send()
        adj_peer_copy(lax.rem(mz + i, nz)).wait_send()


def body(field_in, cotangent, tile_vals, tile_rows, tile_cols, lag_steps, ar_coef):
    n = lax.axis_size("srow")
    row_index = lax.axis_index("srow")
    col_index = lax.axis_index("scol")
    tiles = tile_vals.shape[1]
    cols = field_in.shape[1]
    ncb = cols // BS
    hours = n * TD
    rows = tile_rows[0] - row_index * RBD
    own_cols = lax.dynamic_slice_in_dim(tile_cols, row_index, 1, 0)[0] - col_index * ncb
    place = jnp.arange(tiles, dtype=jnp.int32)
    earlier = place[None, :] < place[:, None]

    def chain(ids, blocks):
        same = (ids[:, None] == ids[None, :]) & earlier
        prev = jnp.max(jnp.where(same, place[None, :] + 1, 0), axis=1)
        which = jnp.arange(blocks, dtype=jnp.int32)[:, None] == ids[None, :]
        last = jnp.max(jnp.where(which, place[None, :] + 1, 0), axis=1)
        return prev, last

    prow, lrow = chain(rows, RBD)
    pcol, lcol = chain(own_cols, ncb)
    idx = jnp.concatenate([rows, own_cols, prow, pcol, lrow, lcol, lag_steps])
    padded = jnp.pad(ar_coef, ((0, 0), (0, MAXLAG)))
    ahead = lax.dynamic_slice_in_dim(padded[1], lag_steps[0], hours)
    spare = jnp.zeros((3, hours), F32)
    coef = jnp.concatenate([ar_coef, ahead[None], padded[2:3, MAXLAG:], spare]).T

    anyspace = pl.BlockSpec(memory_space=pl.ANY)
    vmem = pl.BlockSpec(memory_space=pltpu.VMEM)
    half = hours // 2
    nz = n // PAIR
    wide = RBD * BS
    return pl.pallas_call(
        functools.partial(kernel, n, tiles, ncb),
        out_shape=(
            jax.ShapeDtypeStruct((half, wide), F32),
            jax.ShapeDtypeStruct((TD, cols), F32),
        ),
        in_specs=[pl.BlockSpec(memory_space=pltpu.SMEM), vmem, anyspace, anyspace, anyspace],
        out_specs=(vmem, vmem),
        scratch_shapes=[
            pltpu.VMEM((ncb, hours, BS), BF16),
            pltpu.VMEM((TD, cols), BF16),
            pltpu.VMEM((ncb, TD, BS), BF16),
            pltpu.VMEM((hours, wide), BF16),
            pltpu.VMEM((tiles, BS, BS), BF16),
            pltpu.VMEM((RBD, hours, BS), BF16),
            pltpu.VMEM((tiles + 1, hours, BS), F32),
            pltpu.VMEM((half, cols), F32),
            pltpu.VMEM((half, cols), BF16),
            pltpu.VMEM((half, cols), BF16),
            pltpu.VMEM((half, cols), BF16),
            pltpu.VMEM((half, cols), BF16),
            pltpu.VMEM((hours + MAXLAG, wide), F32),
            pltpu.VMEM((half + MAXLAG, wide), F32),
            pltpu.SemaphoreType.DMA((3,)),
            pltpu.SemaphoreType.DMA((n,)),
            pltpu.SemaphoreType.DMA((n,)),
            pltpu.SemaphoreType.DMA((nz,)),
            pltpu.SemaphoreType.DMA((nz,)),
            pltpu.SemaphoreType.DMA((nz,)),
            pltpu.SemaphoreType.DMA((nz,)),
            pltpu.SemaphoreType.DMA((nz,)),
            pltpu.SemaphoreType.DMA,
            pltpu.SemaphoreType.DMA,
        ],
        compiler_params=pltpu.CompilerParams(
            collective_id=0, has_side_effects=True, vmem_limit_bytes=58 * 1024 * 1024
        ),
        cost_estimate=pl.CostEstimate(
            flops=4 * tiles * hours * BS * BS, bytes_accessed=2 << 20, transcendentals=0
        ),
    )(idx, coef, field_in, cotangent, tile_vals[0])


def solution(mesh):
    in_specs = (
        P(("groups", "srow"), "scol"),
        P("groups", "srow"),
        P(("groups", "srow"), "scol", None, None),
        P(("groups", "srow"), "scol"),
        P("groups", "scol"),
        P("groups"),
        P("groups", None),
    )
    out_specs = (P(("groups", "scol"), "srow"), P(("groups", "srow"), "scol"))
    return jax.shard_map(body, mesh=mesh, in_specs=in_specs, out_specs=out_specs, check_vma=False)
```

```python
import functools

import jax
import jax.numpy as jnp
from jax import lax
from jax.experimental import pallas as pl
from jax.experimental.pallas import tpu as pltpu
from jax.sharding import PartitionSpec as P

BS = 128
RBD = 4
TD = 16
MAXLAG = 24
PAIR = 2
F32 = jnp.float32
BF16 = jnp.bfloat16
MESH = pl.DeviceIdType.MESH


def iotas(rows, cols):
    shape = (rows, cols)
    return lax.broadcasted_iota(jnp.int32, shape, 0), lax.broadcasted_iota(jnp.int32, shape, 1)


def shift_matrix(rows, cols, lag):
    at = lax.broadcasted_iota(jnp.int32, (rows, cols), 0) + lag
    return (lax.broadcasted_iota(jnp.int32, (rows, cols), 1) == at).astype(F32).astype(BF16)


def kernel(
    n,
    tiles,
    ncb,
    field,
    cot,
    mats,
    tile_rows,
    tile_cols,
    lags,
    ar_coef,
    fwd_out,
    adj_out,
    rows_v,
    cols_v,
    lags_s,
    coef_v,
    coef,
    idx_v,
    idx,
    field_all,
    field_v,
    field_send,
    cot_v,
    mats_v,
    adj_in,
    sums,
    adj_part,
    adj_send,
    adj_recv,
    line_send,
    line_recv,
    part,
    part_recv,
    local_sem,
    fs_sem,
    fr_sem,
    fp_sem,
    as_sem,
    ar_sem,
    ls_sem,
    lr_sem,
    ps_sem,
    pr_sem,
):
    hours = n * TD
    half = hours // 2
    ext = half + MAXLAG
    me = lax.axis_index("srow")
    mc = lax.axis_index("scol")
    small = [
        pltpu.make_async_copy(src, dst, local_sem.at[3 + i])
        for i, (src, dst) in enumerate(
            ((tile_rows, rows_v), (tile_cols, cols_v), (lags, lags_s), (ar_coef, coef_v))
        )
    ]
    load_cot = pltpu.make_async_copy(cot, cot_v, local_sem.at[0])
    load_mats = pltpu.make_async_copy(mats, mats_v, local_sem.at[1])
    my_rows = pl.ds(pl.multiple_of(me * TD, TD), TD)
    load_own = pltpu.make_async_copy(field, field_v, local_sem.at[2])
    load_own.start()
    for copy in small:
        copy.start()
    load_cot.start()
    load_mats.start()

    nz = n // PAIR
    mz, my = me // PAIR, lax.rem(me, PAIR)
    peer = mz * PAIR + 1 - my

    def on_line(z):
        return lax.rem(mz + z + nz, nz) * PAIR + my

    barrier = pltpu.get_barrier_semaphore()
    for i in range(1, nz):
        pl.semaphore_signal(barrier, inc=1, device_id={"srow": on_line(i)}, device_id_type=MESH)
    pl.semaphore_signal(barrier, inc=1, device_id={"srow": peer}, device_id_type=MESH)
    pl.semaphore_signal(barrier, inc=1, device_id={"scol": 1 - mc}, device_id_type=MESH)
    load_own.wait()
    for b in range(ncb):
        block = field_v[:, b * BS : (b + 1) * BS]
        field_send[b] = block
        field_all[b, my_rows, :] = block
    for copy in small:
        copy.wait()
    lag1 = lags_s[0]
    at_row, at_col = iotas(n, tiles)
    own_cols = jnp.sum(jnp.where(at_row == me, cols_v[...], 0), 0, keepdims=True)
    table = [
        jnp.clip(rows_v[...] - me * RBD, 0, RBD - 1),
        jnp.clip(own_cols - mc * ncb, 0, ncb - 1),
    ]
    at_row, at_col = iotas(tiles, tiles)
    for ids in (table[0], table[1]):
        column = jnp.sum(jnp.where(at_row == at_col, ids, 0), 1, keepdims=True)
        same = (column == ids) & (at_row < at_col)
        table.append(jnp.max(jnp.where(same, at_row + 1, 0), 0, keepdims=True))
        block_row, block = iotas(tiles, BS)
        table.append(jnp.max(jnp.where(column == block, block_row + 1, 0), 0, keepdims=True))
    idx_v[...] = jnp.zeros_like(idx_v)
    for i, row in enumerate(table):
        idx_v[i : i + 1, 0 : row.shape[1]] = row
    place = pltpu.make_async_copy(idx_v, idx, local_sem.at[7])
    place.start()
    at_row, at_col = iotas(hours, hours)
    terms = ((0, 0), (1, 0), (2, 0), (1, lag1), (2, MAXLAG))
    for i, (term, lag) in enumerate(terms):
        line = jnp.where(at_col == at_row + lag, coef_v[term : term + 1, :], 0.0)
        coef[:, i : i + 1] = jnp.sum(line, 1, keepdims=True)
    pl.semaphore_wait(barrier, nz + 1)

    def rows_of(r):
        return pl.ds(pl.multiple_of(r * TD, TD), TD)

    def line_copy(dst, src):
        return pltpu.make_async_remote_copy(
            src_ref=field_send,
            dst_ref=field_all.at[:, rows_of(src), :],
            send_sem=fs_sem.at[dst],
            recv_sem=fr_sem.at[src],
            device_id={"srow": dst},
            device_id_type=MESH,
        )

    def peer_copy(src):
        return pltpu.make_async_remote_copy(
            src_ref=field_all.at[:, rows_of(src), :],
            dst_ref=field_all.at[:, rows_of(src), :],
            send_sem=fp_sem.at[src // PAIR],
            recv_sem=fr_sem.at[src],
            device_id={"srow": peer},
            device_id_type=MESH,
        )

    def adj_peer_copy(z):
        return pltpu.make_async_remote_copy(
            src_ref=adj_send.at[rows_of(z), :],
            dst_ref=adj_recv.at[rows_of(z), :],
            send_sem=as_sem.at[z],
            recv_sem=ar_sem.at[z],
            device_id={"srow": peer},
            device_id_type=MESH,
        )

    def adj_line_copy(dst, src):
        return pltpu.make_async_remote_copy(
            src_ref=line_send.at[rows_of(dst // PAIR), :],
            dst_ref=line_recv.at[rows_of(src // PAIR), :],
            send_sem=ls_sem.at[dst // PAIR],
            recv_sem=lr_sem.at[src // PAIR],
            device_id={"srow": dst},
            device_id_type=MESH,
        )

    for i in range(1, nz):
        line_copy(on_line(i), me).start()
    peer_copy(me).start()

    load_cot.wait()
    spread = coef[...]
    early = cot_v[...]
    wide = early.astype(F32)
    later = jnp.dot(shift_matrix(hours, hours, lag1), early, preferred_element_type=F32)
    far = jnp.concatenate([wide[MAXLAG:], jnp.zeros((MAXLAG, RBD * BS), F32)], 0)
    adjoint = (
        spread[:, 0:1] * wide + spread[:, 3:4] * later + spread[:, 4:5] * far
    ).astype(BF16)
    for r in range(RBD):
        adj_in[r] = adjoint[:, r * BS : (r + 1) * BS]

    place.wait()
    load_mats.wait()
    sums[0] = jnp.zeros((hours, BS), F32)

    def adj_step(k, carry):
        product = jnp.dot(adj_in[idx[0, k]], mats_v[k], preferred_element_type=F32)
        sums[k + 1] = sums[idx[4, k]] + product
        return carry

    lax.fori_loop(0, tiles, adj_step, 0, unroll=4)
    for b in range(ncb):
        block = sums[idx[5, b]].reshape(nz, PAIR, TD, BS)
        at = slice(b * BS, (b + 1) * BS)
        mine = jnp.where(my == 0, block[:, 0], block[:, 1])
        other = jnp.where(my == 0, block[:, 1], block[:, 0])
        adj_part[:, at] = mine.reshape(half, BS)
        adj_send[:, at] = other.reshape(half, BS).astype(BF16)
    for i in range(1, nz + 1):
        adj_peer_copy(lax.rem(mz + i, nz)).start()
    for i in range(1, nz):
        line_copy(me, on_line(-i)).wait_recv()
        peer_copy(on_line(-i)).start()

    for i in range(1, nz):
        z = lax.rem(mz + i, nz)
        adj_peer_copy(z).wait_recv()
        total = adj_part[rows_of(z), :] + adj_recv[rows_of(z), :].astype(F32)
        line_send[rows_of(z), :] = total.astype(BF16)
        adj_line_copy(on_line(i), me).start()

    for i in range(nz):
        peer_copy(lax.rem(mz + nz - i, nz) * PAIR + 1 - my).wait_recv()

    def fwd_step(k, carry):
        product = lax.dot_general(
            field_all[idx[1, k]], mats_v[k], (((1,), (1,)), ((), ())), preferred_element_type=F32
        )
        sums[k + 1] = sums[idx[2, k]] + product
        return carry

    lax.fori_loop(0, tiles, fwd_step, 0, unroll=4)
    part[pl.ds(0, MAXLAG), :] = jnp.zeros((MAXLAG, RBD * BS), F32)
    for r in range(RBD):
        part[pl.ds(MAXLAG, hours), r * BS : (r + 1) * BS] = sums[idx[3, r]]
    exchange = pltpu.make_async_remote_copy(
        src_ref=part.at[pl.ds(pl.multiple_of((1 - mc) * half, 8), ext), :],
        dst_ref=part_recv,
        send_sem=ps_sem,
        recv_sem=pr_sem,
        device_id={"scol": 1 - mc},
        device_id_type=MESH,
    )
    exchange.start()
    exchange.wait_recv()
    own = part[pl.ds(pl.multiple_of(mc * half, 8), ext), :]
    value = (own + part_recv[...]).astype(BF16)
    spread = coef[pl.ds(pl.multiple_of(mc * half, 8), half), :]
    delayed = jnp.dot(
        shift_matrix(half, ext, MAXLAG - lag1), value, preferred_element_type=F32
    )
    value = value.astype(F32)
    fwd_out[...] = (
        spread[:, 0:1] * value[MAXLAG:] + spread[:, 1:2] * delayed + spread[:, 2:3] * value[:half]
    )

    adj_peer_copy(mz).wait_recv()
    total = adj_part[rows_of(mz), :] + adj_recv[rows_of(mz), :].astype(F32)
    for i in range(1, nz):
        src = on_line(-i)
        adj_line_copy(me, src).wait_recv()
        total += line_recv[rows_of(src // PAIR), :].astype(F32)
    adj_out[...] = total

    exchange.wait_send()
    for i in range(1, nz):
        line_copy(on_line(i), me).wait_send()
        adj_line_copy(on_line(i), me).wait_send()
    for i in range(nz):
        peer_copy(on_line(-i)).wait_send()
        adj_peer_copy(lax.rem(mz + i, nz)).wait_send()


def body(field_in, cotangent, tile_vals, tile_rows, tile_cols, lag_steps, ar_coef):
    n = lax.axis_size("srow")
    tiles = tile_vals.shape[1]
    cols = field_in.shape[1]
    ncb = cols // BS
    hours = n * TD
    anyspace = pl.BlockSpec(memory_space=pl.ANY)
    vmem = pl.BlockSpec(memory_space=pltpu.VMEM)
    half = hours // 2
    nz = n // PAIR
    wide = RBD * BS
    return pl.pallas_call(
        functools.partial(kernel, n, tiles, ncb),
        out_shape=(
            jax.ShapeDtypeStruct((half, wide), F32),
            jax.ShapeDtypeStruct((TD, cols), F32),
        ),
        in_specs=[anyspace] * 7,
        out_specs=(vmem, vmem),
        scratch_shapes=[
            pltpu.VMEM((1, tiles), jnp.int32),
            pltpu.VMEM((n, tiles), jnp.int32),
            pltpu.SMEM((2,), jnp.int32),
            pltpu.VMEM((3, hours), F32),
            pltpu.VMEM((hours, 8), F32),
            pltpu.VMEM((8, BS), jnp.int32),
            pltpu.SMEM((8, BS), jnp.int32),
            pltpu.VMEM((ncb, hours, BS), BF16),
            pltpu.VMEM((TD, cols), BF16),
            pltpu.VMEM((ncb, TD, BS), BF16),
            pltpu.VMEM((hours, wide), BF16),
            pltpu.VMEM((tiles, BS, BS), BF16),
            pltpu.VMEM((RBD, hours, BS), BF16),
            pltpu.VMEM((tiles + 1, hours, BS), F32),
            pltpu.VMEM((half, cols), F32),
            pltpu.VMEM((half, cols), BF16),
            pltpu.VMEM((half, cols), BF16),
            pltpu.VMEM((half, cols), BF16),
            pltpu.VMEM((half, cols), BF16),
            pltpu.VMEM((hours + MAXLAG, wide), F32),
            pltpu.VMEM((half + MAXLAG, wide), F32),
            pltpu.SemaphoreType.DMA((8,)),
            pltpu.SemaphoreType.DMA((n,)),
            pltpu.SemaphoreType.DMA((n,)),
            pltpu.SemaphoreType.DMA((nz,)),
            pltpu.SemaphoreType.DMA((nz,)),
            pltpu.SemaphoreType.DMA((nz,)),
            pltpu.SemaphoreType.DMA((nz,)),
            pltpu.SemaphoreType.DMA((nz,)),
            pltpu.SemaphoreType.DMA,
            pltpu.SemaphoreType.DMA,
        ],
        compiler_params=pltpu.CompilerParams(
            collective_id=0, has_side_effects=True, vmem_limit_bytes=58 * 1024 * 1024
        ),
        cost_estimate=pl.CostEstimate(
            flops=4 * tiles * hours * BS * BS, bytes_accessed=2 << 20, transcendentals=0
        ),
    )(field_in, cotangent, tile_vals[0], tile_rows, tile_cols, lag_steps, ar_coef)


def solution(mesh):
    in_specs = (
        P(("groups", "srow"), "scol"),
        P("groups", "srow"),
        P(("groups", "srow"), "scol", None, None),
        P(("groups", "srow"), "scol"),
        P("groups", "scol"),
        P("groups"),
        P("groups", None),
    )
    out_specs = (P(("groups", "scol"), "srow"), P(("groups", "srow"), "scol"))
    return jax.shard_map(body, mesh=mesh, in_specs=in_specs, out_specs=out_specs, check_vma=False)
```

```python
import functools

import jax
import jax.numpy as jnp
from jax import lax
from jax.experimental import pallas as pl
from jax.experimental.pallas import tpu as pltpu
from jax.sharding import PartitionSpec as P

BS = 128
RBD = 4
TD = 16
MAXLAG = 24
PAIR = 2
F32 = jnp.float32
BF16 = jnp.bfloat16
MESH = pl.DeviceIdType.MESH


def iotas(rows, cols):
    shape = (rows, cols)
    return lax.broadcasted_iota(jnp.int32, shape, 0), lax.broadcasted_iota(jnp.int32, shape, 1)


def shift_matrix(rows, cols, lag):
    at = lax.broadcasted_iota(jnp.int32, (rows, cols), 0) + lag
    return (lax.broadcasted_iota(jnp.int32, (rows, cols), 1) == at).astype(F32).astype(BF16)


def kernel(
    n,
    tiles,
    ncb,
    field,
    cot,
    mats,
    tile_rows,
    tile_cols,
    lags,
    ar_coef,
    fwd_out,
    adj_out,
    rows_v,
    cols_v,
    lags_s,
    coef_v,
    coef,
    idx_v,
    idx,
    field_all,
    field_v,
    field_send,
    cot_v,
    mats_v,
    adj_in,
    sums,
    adj_part,
    adj_send,
    adj_recv,
    line_send,
    line_recv,
    part,
    part_recv,
    local_sem,
    fs_sem,
    fr_sem,
    fp_sem,
    as_sem,
    ar_sem,
    ls_sem,
    lr_sem,
    ps_sem,
    pr_sem,
):
    hours = n * TD
    half = hours // 2
    ext = half + MAXLAG
    me = lax.axis_index("srow")
    mc = lax.axis_index("scol")
    small = [
        pltpu.make_async_copy(src, dst, local_sem.at[3 + i])
        for i, (src, dst) in enumerate(
            ((tile_rows, rows_v), (tile_cols, cols_v), (lags, lags_s), (ar_coef, coef_v))
        )
    ]
    load_cot = pltpu.make_async_copy(cot, cot_v, local_sem.at[0])
    load_mats = pltpu.make_async_copy(mats, mats_v, local_sem.at[1])
    my_rows = pl.ds(pl.multiple_of(me * TD, TD), TD)
    load_own = pltpu.make_async_copy(field, field_v, local_sem.at[2])
    load_own.start()
    for copy in small:
        copy.start()
    load_cot.start()
    load_mats.start()

    nz = n // PAIR
    mz, my = me // PAIR, lax.rem(me, PAIR)
    peer = mz * PAIR + 1 - my

    def on_line(z):
        return lax.rem(mz + z + nz, nz) * PAIR + my

    barrier = pltpu.get_barrier_semaphore()
    for i in range(1, nz):
        pl.semaphore_signal(barrier, inc=1, device_id={"srow": on_line(i)}, device_id_type=MESH)
    pl.semaphore_signal(barrier, inc=1, device_id={"srow": peer}, device_id_type=MESH)
    pl.semaphore_signal(barrier, inc=1, device_id={"scol": 1 - mc}, device_id_type=MESH)
    load_own.wait()
    for b in range(ncb):
        block = field_v[:, b * BS : (b + 1) * BS]
        field_send[b] = block
        field_all[b, my_rows, :] = block
    for copy in small:
        copy.wait()
    lag1 = lags_s[0]
    at_row, at_col = iotas(n, tiles)
    own_cols = jnp.sum(jnp.where(at_row == me, cols_v[...], 0), 0, keepdims=True)
    table = [
        jnp.clip(rows_v[...] - me * RBD, 0, RBD - 1),
        jnp.clip(own_cols - mc * ncb, 0, ncb - 1),
    ]
    at_row, at_col = iotas(tiles, tiles)
    for ids in (table[0], table[1]):
        column = jnp.sum(jnp.where(at_row == at_col, ids, 0), 1, keepdims=True)
        same = (column == ids) & (at_row < at_col)
        table.append(jnp.max(jnp.where(same, at_row + 1, 0), 0, keepdims=True))
        block_row, block = iotas(tiles, BS)
        table.append(jnp.max(jnp.where(column == block, block_row + 1, 0), 0, keepdims=True))
    idx_v[...] = jnp.zeros_like(idx_v)
    for i, row in enumerate(table):
        idx_v[i : i + 1, 0 : row.shape[1]] = row
    place = pltpu.make_async_copy(idx_v, idx, local_sem.at[7])
    place.start()
    at_row, at_col = iotas(hours, hours)
    terms = ((0, 0), (1, 0), (2, 0), (1, lag1), (2, MAXLAG))
    for i, (term, lag) in enumerate(terms):
        line = jnp.where(at_col == at_row + lag, coef_v[term : term + 1, :], 0.0)
        coef[:, i : i + 1] = jnp.sum(line, 1, keepdims=True)
    pl.semaphore_wait(barrier, nz + 1)

    def rows_of(r):
        return pl.ds(pl.multiple_of(r * TD, TD), TD)

    def line_copy(dst, src):
        return pltpu.make_async_remote_copy(
            src_ref=field_send,
            dst_ref=field_all.at[:, rows_of(src), :],
            send_sem=fs_sem.at[dst],
            recv_sem=fr_sem.at[src],
            device_id={"srow": dst},
            device_id_type=MESH,
        )

    def peer_copy(src):
        return pltpu.make_async_remote_copy(
            src_ref=field_all.at[:, rows_of(src), :],
            dst_ref=field_all.at[:, rows_of(src), :],
            send_sem=fp_sem.at[src // PAIR],
            recv_sem=fr_sem.at[src],
            device_id={"srow": peer},
            device_id_type=MESH,
        )

    def adj_peer_copy(z):
        return pltpu.make_async_remote_copy(
            src_ref=adj_send.at[rows_of(z), :],
            dst_ref=adj_recv.at[rows_of(z), :],
            send_sem=as_sem.at[z],
            recv_sem=ar_sem.at[z],
            device_id={"srow": peer},
            device_id_type=MESH,
        )

    def adj_line_copy(dst, src):
        return pltpu.make_async_remote_copy(
            src_ref=line_send.at[rows_of(dst // PAIR), :],
            dst_ref=line_recv.at[rows_of(src // PAIR), :],
            send_sem=ls_sem.at[dst // PAIR],
            recv_sem=lr_sem.at[src // PAIR],
            device_id={"srow": dst},
            device_id_type=MESH,
        )

    for i in range(1, nz):
        line_copy(on_line(i), me).start()
    peer_copy(me).start()

    load_cot.wait()
    spread = coef[...]
    early = cot_v[...]
    wide = early.astype(F32)
    later = jnp.dot(shift_matrix(hours, hours, lag1), early, preferred_element_type=F32)
    far = jnp.concatenate([wide[MAXLAG:], jnp.zeros((MAXLAG, RBD * BS), F32)], 0)
    adjoint = (
        spread[:, 0:1] * wide + spread[:, 3:4] * later + spread[:, 4:5] * far
    ).astype(BF16)
    for r in range(RBD):
        adj_in[r] = adjoint[:, r * BS : (r + 1) * BS]

    place.wait()
    load_mats.wait()
    sums[0] = jnp.zeros((hours, BS), F32)

    def adj_step(k, carry):
        product = jnp.dot(adj_in[idx[0, k]], mats_v[k], preferred_element_type=F32)
        sums[k + 1] = sums[idx[4, k]] + product
        return carry

    lax.fori_loop(0, tiles, adj_step, 0, unroll=4)
    for b in range(ncb):
        block = sums[idx[5, b]].reshape(nz, PAIR, TD, BS)
        at = slice(b * BS, (b + 1) * BS)
        mine = jnp.where(my == 0, block[:, 0], block[:, 1])
        other = jnp.where(my == 0, block[:, 1], block[:, 0])
        adj_part[:, at] = mine.reshape(half, BS)
        adj_send[:, at] = other.reshape(half, BS).astype(BF16)
    for i in range(1, nz + 1):
        adj_peer_copy(lax.rem(mz + i, nz)).start()
    for i in range(1, nz):
        line_copy(me, on_line(-i)).wait_recv()
        peer_copy(on_line(-i)).start()

    for i in range(1, nz):
        z = lax.rem(mz + i, nz)
        adj_peer_copy(z).wait_recv()
        total = adj_part[rows_of(z), :] + adj_recv[rows_of(z), :].astype(F32)
        line_send[rows_of(z), :] = total.astype(BF16)
        adj_line_copy(on_line(i), me).start()

    for i in range(nz):
        peer_copy(lax.rem(mz + nz - i, nz) * PAIR + 1 - my).wait_recv()

    def fwd_step(k, carry):
        product = lax.dot_general(
            field_all[idx[1, k]], mats_v[k], (((1,), (1,)), ((), ())), preferred_element_type=F32
        )
        sums[k + 1] = sums[idx[2, k]] + product
        return carry

    lax.fori_loop(0, tiles, fwd_step, 0, unroll=4)
    part[pl.ds(0, MAXLAG), :] = jnp.zeros((MAXLAG, RBD * BS), F32)
    for r in range(RBD):
        part[pl.ds(MAXLAG, hours), r * BS : (r + 1) * BS] = sums[idx[3, r]]
    exchange = pltpu.make_async_remote_copy(
        src_ref=part.at[pl.ds(pl.multiple_of((1 - mc) * half, 8), ext), :],
        dst_ref=part_recv,
        send_sem=ps_sem,
        recv_sem=pr_sem,
        device_id={"scol": 1 - mc},
        device_id_type=MESH,
    )
    exchange.start()
    exchange.wait_recv()
    own = part[pl.ds(pl.multiple_of(mc * half, 8), ext), :]
    value = (own + part_recv[...]).astype(BF16)
    spread = coef[pl.ds(pl.multiple_of(mc * half, 8), half), :]
    delayed = jnp.dot(
        shift_matrix(half, ext, MAXLAG - lag1), value, preferred_element_type=F32
    )
    value = value.astype(F32)
    fwd_out[...] = (
        spread[:, 0:1] * value[MAXLAG:] + spread[:, 1:2] * delayed + spread[:, 2:3] * value[:half]
    )

    adj_peer_copy(mz).wait_recv()
    total = adj_part[rows_of(mz), :] + adj_recv[rows_of(mz), :].astype(F32)
    for i in range(1, nz):
        src = on_line(-i)
        adj_line_copy(me, src).wait_recv()
        total += line_recv[rows_of(src // PAIR), :].astype(F32)
    adj_out[...] = total

    exchange.wait_send()
    for i in range(1, nz):
        line_copy(on_line(i), me).wait_send()
        adj_line_copy(on_line(i), me).wait_send()
    for i in range(nz):
        peer_copy(on_line(-i)).wait_send()
        adj_peer_copy(lax.rem(mz + i, nz)).wait_send()


def hand_over(fwd, adj, fwd_out, adj_out, sem):
    first = pltpu.make_async_copy(fwd, fwd_out, sem.at[0])
    second = pltpu.make_async_copy(adj, adj_out, sem.at[1])
    first.start()
    second.start()
    first.wait()
    second.wait()


def body(field_in, cotangent, tile_vals, tile_rows, tile_cols, lag_steps, ar_coef):
    n = lax.axis_size("srow")
    tiles = tile_vals.shape[1]
    cols = field_in.shape[1]
    ncb = cols // BS
    hours = n * TD
    anyspace = pl.BlockSpec(memory_space=pl.ANY)
    vmem = pl.BlockSpec(memory_space=pltpu.VMEM)
    half = hours // 2
    nz = n // PAIR
    wide = RBD * BS
    results = pl.pallas_call(
        functools.partial(kernel, n, tiles, ncb),
        out_shape=(
            jax.ShapeDtypeStruct((half, wide), F32),
            jax.ShapeDtypeStruct((TD, cols), F32),
        ),
        in_specs=[anyspace] * 7,
        out_specs=(vmem, vmem),
        scratch_shapes=[
            pltpu.VMEM((1, tiles), jnp.int32),
            pltpu.VMEM((n, tiles), jnp.int32),
            pltpu.SMEM((2,), jnp.int32),
            pltpu.VMEM((3, hours), F32),
            pltpu.VMEM((hours, 8), F32),
            pltpu.VMEM((8, BS), jnp.int32),
            pltpu.SMEM((8, BS), jnp.int32),
            pltpu.VMEM((ncb, hours, BS), BF16),
            pltpu.VMEM((TD, cols), BF16),
            pltpu.VMEM((ncb, TD, BS), BF16),
            pltpu.VMEM((hours, wide), BF16),
            pltpu.VMEM((tiles, BS, BS), BF16),
            pltpu.VMEM((RBD, hours, BS), BF16),
            pltpu.VMEM((tiles + 1, hours, BS), F32),
            pltpu.VMEM((half, cols), F32),
            pltpu.VMEM((half, cols), BF16),
            pltpu.VMEM((half, cols), BF16),
            pltpu.VMEM((half, cols), BF16),
            pltpu.VMEM((half, cols), BF16),
            pltpu.VMEM((hours + MAXLAG, wide), F32),
            pltpu.VMEM((half + MAXLAG, wide), F32),
            pltpu.SemaphoreType.DMA((8,)),
            pltpu.SemaphoreType.DMA((n,)),
            pltpu.SemaphoreType.DMA((n,)),
            pltpu.SemaphoreType.DMA((nz,)),
            pltpu.SemaphoreType.DMA((nz,)),
            pltpu.SemaphoreType.DMA((nz,)),
            pltpu.SemaphoreType.DMA((nz,)),
            pltpu.SemaphoreType.DMA((nz,)),
            pltpu.SemaphoreType.DMA,
            pltpu.SemaphoreType.DMA,
        ],
        compiler_params=pltpu.CompilerParams(
            collective_id=0, has_side_effects=True, vmem_limit_bytes=58 * 1024 * 1024
        ),
        cost_estimate=pl.CostEstimate(
            flops=4 * tiles * hours * BS * BS, bytes_accessed=2 << 20, transcendentals=0
        ),
    )(field_in, cotangent, tile_vals[0], tile_rows, tile_cols, lag_steps, ar_coef)
    return pl.pallas_call(
        hand_over,
        out_shape=[jax.ShapeDtypeStruct(value.shape, F32) for value in results],
        in_specs=[anyspace] * 2,
        out_specs=[anyspace] * 2,
        scratch_shapes=[pltpu.SemaphoreType.DMA((2,))],
    )(*results)


def solution(mesh):
    in_specs = (
        P(("groups", "srow"), "scol"),
        P("groups", "srow"),
        P(("groups", "srow"), "scol", None, None),
        P(("groups", "srow"), "scol"),
        P("groups", "scol"),
        P("groups"),
        P("groups", None),
    )
    out_specs = (P(("groups", "scol"), "srow"), P(("groups", "srow"), "scol"))
    return jax.shard_map(body, mesh=mesh, in_specs=in_specs, out_specs=out_specs, check_vma=False)
```

```python
import functools

import jax
import jax.numpy as jnp
from jax import lax
from jax.experimental import pallas as pl
from jax.experimental.pallas import tpu as pltpu
from jax.sharding import PartitionSpec as P

BS = 128
RBD = 4
TD = 16
MAXLAG = 24
PAIR = 2
F32 = jnp.float32
BF16 = jnp.bfloat16
MESH = pl.DeviceIdType.MESH


def iotas(rows, cols):
    shape = (rows, cols)
    return lax.broadcasted_iota(jnp.int32, shape, 0), lax.broadcasted_iota(jnp.int32, shape, 1)


def shift_matrix(rows, cols, lag):
    at = lax.broadcasted_iota(jnp.int32, (rows, cols), 0) + lag
    return (lax.broadcasted_iota(jnp.int32, (rows, cols), 1) == at).astype(F32).astype(BF16)


def kernel(
    n,
    tiles,
    ncb,
    field,
    cot,
    mats,
    tile_rows,
    tile_cols,
    lags,
    ar_coef,
    fwd_out,
    adj_out,
    rows_v,
    cols_v,
    lags_s,
    coef_v,
    coef,
    idx_v,
    idx,
    field_all,
    field_v,
    cot_v,
    mats_v,
    adj_in,
    sums,
    adj_part,
    adj_send,
    adj_recv,
    line_send,
    line_recv,
    part,
    part_recv,
    local_sem,
    fs_sem,
    fr_sem,
    fp_sem,
    as_sem,
    ar_sem,
    ls_sem,
    lr_sem,
    ps_sem,
    pr_sem,
):
    hours = n * TD
    half = hours // 2
    ext = half + MAXLAG
    me = lax.axis_index("srow")
    mc = lax.axis_index("scol")
    small = [
        pltpu.make_async_copy(src, dst, local_sem.at[3 + i])
        for i, (src, dst) in enumerate(
            ((tile_rows, rows_v), (tile_cols, cols_v), (lags, lags_s), (ar_coef, coef_v))
        )
    ]
    load_cot = pltpu.make_async_copy(cot, cot_v, local_sem.at[0])
    load_mats = pltpu.make_async_copy(mats, mats_v, local_sem.at[1])
    my_rows = pl.ds(pl.multiple_of(me * TD, TD), TD)
    load_own = pltpu.make_async_copy(field, field_v, local_sem.at[2])
    load_own.start()
    for copy in small:
        copy.start()
    load_cot.start()
    load_mats.start()

    nz = n // PAIR
    mz, my = me // PAIR, lax.rem(me, PAIR)
    peer = mz * PAIR + 1 - my

    def on_line(z):
        return lax.rem(mz + z + nz, nz) * PAIR + my

    barrier = pltpu.get_barrier_semaphore()
    for i in range(1, nz):
        pl.semaphore_signal(barrier, inc=1, device_id={"srow": on_line(i)}, device_id_type=MESH)
    pl.semaphore_signal(barrier, inc=1, device_id={"srow": peer}, device_id_type=MESH)
    pl.semaphore_signal(barrier, inc=1, device_id={"scol": 1 - mc}, device_id_type=MESH)
    load_own.wait()
    for b in range(ncb):
        block = field_v[:, b * BS : (b + 1) * BS]
        field_all[b, my_rows, :] = block
    for copy in small:
        copy.wait()
    lag1 = lags_s[0]
    at_row, at_col = iotas(n, tiles)
    own_cols = jnp.sum(jnp.where(at_row == me, cols_v[...], 0), 0, keepdims=True)
    table = [
        jnp.clip(rows_v[...] - me * RBD, 0, RBD - 1),
        jnp.clip(own_cols - mc * ncb, 0, ncb - 1),
    ]
    at_row, at_col = iotas(tiles, tiles)
    for ids in (table[0], table[1]):
        column = jnp.sum(jnp.where(at_row == at_col, ids, 0), 1, keepdims=True)
        same = (column == ids) & (at_row < at_col)
        table.append(jnp.max(jnp.where(same, at_row + 1, 0), 0, keepdims=True))
        block_row, block = iotas(tiles, BS)
        table.append(jnp.max(jnp.where(column == block, block_row + 1, 0), 0, keepdims=True))
    idx_v[...] = jnp.zeros_like(idx_v)
    for i, row in enumerate(table):
        idx_v[i : i + 1, 0 : row.shape[1]] = row
    place = pltpu.make_async_copy(idx_v, idx, local_sem.at[7])
    place.start()
    at_row, at_col = iotas(hours, hours)
    terms = ((0, 0), (1, 0), (2, 0), (1, lag1), (2, MAXLAG))
    for i, (term, lag) in enumerate(terms):
        line = jnp.where(at_col == at_row + lag, coef_v[term : term + 1, :], 0.0)
        coef[:, i : i + 1] = jnp.sum(line, 1, keepdims=True)
    pl.semaphore_wait(barrier, nz + 1)

    def rows_of(r):
        return pl.ds(pl.multiple_of(r * TD, TD), TD)

    def line_copy(way, src):
        return pltpu.make_async_remote_copy(
            src_ref=field_all.at[:, rows_of(src), :],
            dst_ref=field_all.at[:, rows_of(src), :],
            send_sem=fs_sem.at[(1 + way) // 2 * nz + src // PAIR],
            recv_sem=fr_sem.at[src],
            device_id={"srow": me + way * PAIR},
            device_id_type=MESH,
        )

    def peer_copy(src):
        return pltpu.make_async_remote_copy(
            src_ref=field_all.at[:, rows_of(src), :],
            dst_ref=field_all.at[:, rows_of(src), :],
            send_sem=fp_sem.at[src // PAIR],
            recv_sem=fr_sem.at[src],
            device_id={"srow": peer},
            device_id_type=MESH,
        )

    def adj_peer_copy(z):
        return pltpu.make_async_remote_copy(
            src_ref=adj_send.at[rows_of(z), :],
            dst_ref=adj_recv.at[rows_of(z), :],
            send_sem=as_sem.at[z],
            recv_sem=ar_sem.at[z],
            device_id={"srow": peer},
            device_id_type=MESH,
        )

    def adj_line_copy(dst, src):
        return pltpu.make_async_remote_copy(
            src_ref=line_send.at[rows_of(dst // PAIR), :],
            dst_ref=line_recv.at[rows_of(src // PAIR), :],
            send_sem=ls_sem.at[dst // PAIR],
            recv_sem=lr_sem.at[src // PAIR],
            device_id={"srow": dst},
            device_id_type=MESH,
        )

    ways = (1, -1)

    def arrival(step, way, act):
        z = mz - way * step
        pl.when((z >= 0) & (z < nz))(lambda: act(z * PAIR + my))

    def onward(src, way, act):
        z = mz + way
        pl.when((z >= 0) & (z < nz))(lambda: act(line_copy(way, src)))

    def pass_on(step):
        for way in ways:

            def act(src, way=way):
                line_copy(way, src).wait_recv()
                onward(src, way, lambda copy: copy.start())
                peer_copy(src).start()

            arrival(step, way, act)

    for way in ways:
        onward(me, way, lambda copy: copy.start())
    peer_copy(me).start()

    load_cot.wait()
    spread = coef[...]
    early = cot_v[...]
    wide = early.astype(F32)
    later = jnp.dot(shift_matrix(hours, hours, lag1), early, preferred_element_type=F32)
    far = jnp.concatenate([wide[MAXLAG:], jnp.zeros((MAXLAG, RBD * BS), F32)], 0)
    adjoint = (
        spread[:, 0:1] * wide + spread[:, 3:4] * later + spread[:, 4:5] * far
    ).astype(BF16)
    for r in range(RBD):
        adj_in[r] = adjoint[:, r * BS : (r + 1) * BS]

    place.wait()
    load_mats.wait()
    sums[0] = jnp.zeros((hours, BS), F32)

    def adj_step(k, carry):
        product = jnp.dot(adj_in[idx[0, k]], mats_v[k], preferred_element_type=F32)
        sums[k + 1] = sums[idx[4, k]] + product
        return carry

    lax.fori_loop(0, tiles // 2, adj_step, 0, unroll=4)
    pass_on(1)
    lax.fori_loop(tiles // 2, tiles, adj_step, 0, unroll=4)
    for b in range(ncb):
        block = sums[idx[5, b]].reshape(nz, PAIR, TD, BS)
        at = slice(b * BS, (b + 1) * BS)
        mine = jnp.where(my == 0, block[:, 0], block[:, 1])
        other = jnp.where(my == 0, block[:, 1], block[:, 0])
        adj_part[:, at] = mine.reshape(half, BS)
        adj_send[:, at] = other.reshape(half, BS).astype(BF16)
    for i in range(1, nz + 1):
        adj_peer_copy(lax.rem(mz + i, nz)).start()
    for i in range(1, nz):
        if i > 1:
            pass_on(i)

    for i in range(1, nz):
        z = lax.rem(mz + i, nz)
        adj_peer_copy(z).wait_recv()
        total = adj_part[rows_of(z), :] + adj_recv[rows_of(z), :].astype(F32)
        line_send[rows_of(z), :] = total.astype(BF16)
        adj_line_copy(on_line(i), me).start()

    for i in range(nz):
        peer_copy(lax.rem(mz + nz - i, nz) * PAIR + 1 - my).wait_recv()

    def fwd_step(k, carry):
        product = lax.dot_general(
            field_all[idx[1, k]], mats_v[k], (((1,), (1,)), ((), ())), preferred_element_type=F32
        )
        sums[k + 1] = sums[idx[2, k]] + product
        return carry

    lax.fori_loop(0, tiles, fwd_step, 0, unroll=4)
    part[pl.ds(0, MAXLAG), :] = jnp.zeros((MAXLAG, RBD * BS), F32)
    for r in range(RBD):
        part[pl.ds(MAXLAG, hours), r * BS : (r + 1) * BS] = sums[idx[3, r]]
    exchange = pltpu.make_async_remote_copy(
        src_ref=part.at[pl.ds(pl.multiple_of((1 - mc) * half, 8), ext), :],
        dst_ref=part_recv,
        send_sem=ps_sem,
        recv_sem=pr_sem,
        device_id={"scol": 1 - mc},
        device_id_type=MESH,
    )
    exchange.start()
    exchange.wait_recv()
    own = part[pl.ds(pl.multiple_of(mc * half, 8), ext), :]
    value = (own + part_recv[...]).astype(BF16)
    spread = coef[pl.ds(pl.multiple_of(mc * half, 8), half), :]
    delayed = jnp.dot(
        shift_matrix(half, ext, MAXLAG - lag1), value, preferred_element_type=F32
    )
    value = value.astype(F32)
    fwd_out[...] = (
        spread[:, 0:1] * value[MAXLAG:] + spread[:, 1:2] * delayed + spread[:, 2:3] * value[:half]
    )

    adj_peer_copy(mz).wait_recv()
    total = adj_part[rows_of(mz), :] + adj_recv[rows_of(mz), :].astype(F32)
    for i in range(1, nz):
        src = on_line(-i)
        adj_line_copy(me, src).wait_recv()
        total += line_recv[rows_of(src // PAIR), :].astype(F32)
    adj_out[...] = total

    exchange.wait_send()
    for i in range(1, nz):
        adj_line_copy(on_line(i), me).wait_send()
    for way in ways:
        onward(me, way, lambda copy: copy.wait_send())
        for i in range(1, nz):

            def sent(src, way=way):
                onward(src, way, lambda copy: copy.wait_send())

            arrival(i, way, sent)
    for i in range(nz):
        peer_copy(on_line(-i)).wait_send()
        adj_peer_copy(lax.rem(mz + i, nz)).wait_send()


def body(field_in, cotangent, tile_vals, tile_rows, tile_cols, lag_steps, ar_coef):
    n = lax.axis_size("srow")
    tiles = tile_vals.shape[1]
    cols = field_in.shape[1]
    ncb = cols // BS
    hours = n * TD
    anyspace = pl.BlockSpec(memory_space=pl.ANY)
    vmem = pl.BlockSpec(memory_space=pltpu.VMEM)
    half = hours // 2
    nz = n // PAIR
    wide = RBD * BS
    return pl.pallas_call(
        functools.partial(kernel, n, tiles, ncb),
        out_shape=(
            jax.ShapeDtypeStruct((half, wide), F32),
            jax.ShapeDtypeStruct((TD, cols), F32),
        ),
        in_specs=[anyspace] * 7,
        out_specs=(vmem, vmem),
        scratch_shapes=[
            pltpu.VMEM((1, tiles), jnp.int32),
            pltpu.VMEM((n, tiles), jnp.int32),
            pltpu.SMEM((2,), jnp.int32),
            pltpu.VMEM((3, hours), F32),
            pltpu.VMEM((hours, 8), F32),
            pltpu.VMEM((8, BS), jnp.int32),
            pltpu.SMEM((8, BS), jnp.int32),
            pltpu.VMEM((ncb, hours, BS), BF16),
            pltpu.VMEM((TD, cols), BF16),
            pltpu.VMEM((hours, wide), BF16),
            pltpu.VMEM((tiles, BS, BS), BF16),
            pltpu.VMEM((RBD, hours, BS), BF16),
            pltpu.VMEM((tiles + 1, hours, BS), F32),
            pltpu.VMEM((half, cols), F32),
            pltpu.VMEM((half, cols), BF16),
            pltpu.VMEM((half, cols), BF16),
            pltpu.VMEM((half, cols), BF16),
            pltpu.VMEM((half, cols), BF16),
            pltpu.VMEM((hours + MAXLAG, wide), F32),
            pltpu.VMEM((half + MAXLAG, wide), F32),
            pltpu.SemaphoreType.DMA((8,)),
            pltpu.SemaphoreType.DMA((n,)),
            pltpu.SemaphoreType.DMA((n,)),
            pltpu.SemaphoreType.DMA((nz,)),
            pltpu.SemaphoreType.DMA((nz,)),
            pltpu.SemaphoreType.DMA((nz,)),
            pltpu.SemaphoreType.DMA((nz,)),
            pltpu.SemaphoreType.DMA((nz,)),
            pltpu.SemaphoreType.DMA,
            pltpu.SemaphoreType.DMA,
        ],
        compiler_params=pltpu.CompilerParams(
            collective_id=0, has_side_effects=True, vmem_limit_bytes=58 * 1024 * 1024
        ),
        cost_estimate=pl.CostEstimate(
            flops=4 * tiles * hours * BS * BS, bytes_accessed=2 << 20, transcendentals=0
        ),
    )(field_in, cotangent, tile_vals[0], tile_rows, tile_cols, lag_steps, ar_coef)


def solution(mesh):
    in_specs = (
        P(("groups", "srow"), "scol"),
        P("groups", "srow"),
        P(("groups", "srow"), "scol", None, None),
        P(("groups", "srow"), "scol"),
        P("groups", "scol"),
        P("groups"),
        P("groups", None),
    )
    out_specs = (P(("groups", "scol"), "srow"), P(("groups", "srow"), "scol"))
    return jax.shard_map(body, mesh=mesh, in_specs=in_specs, out_specs=out_specs, check_vma=False)
```
